32 devices in a mesh: groups: 2 (over x), grid: 8 (over z, y), layer: 2 (over core).
Axes of the slice: x: 2, y: 2, z: 4, core: 2. Of those that a mesh axis runs over, the one named last changes fastest.
Arguments:
- density: float32 [2048, 1024], P(('groups', 'grid'), 'layer'), parts along dimension 0, as said below
- pattern: int32 [8, 8], replicated, may hold values from 0 to 1, as said below
- branch: int32 [8], replicated, may hold values from 0 to 1
- keep_blocks: int32 [8, 8], replicated, may hold values from 0 to 1, as said below
Outputs:
- purified: float32 [2048, 1024], P(('groups', 'grid'), 'layer'), parts along dimension 0
- occupation: float32 [2], P('groups'), parts along dimension 0
The draws below stay inside these ranges and needn't reach their ends.
There are 2 independent parts, one for each index of `groups`. The reference program is written for one: setup_inputs(seed, part) draws one part's arguments, and reference() takes and returns one part's arrays. A program takes and returns all parts, laid end to end along the dimension named above; an argument that names none is the same for every part. Nothing has to cross between parts.
Inputs may be any that keep to these rules, and one draw needn't show every extreme that they name: density is symmetric. pattern is symmetric, holds only 0 and 1, has ones on its diagonal, and each of its rows holds exactly 3 ones. keep_blocks is symmetric, holds only 0 and 1 and has ones on its diagonal.
All inputs are finite; a program needn't handle non-finite values.
Results may differ from the reference program's by a relative error of at most 0.0003.
Values sent between devices are 32-bit elements; how exact they have to be, the bound alone decides.
A program may use at most 128 MiB of HBM per device.

```python
import jax
import jax.numpy as jnp
from jax import lax

BLOCK = 128
ORDER = 1024
NBLK = 8


def draw_density(key, part):
    key = jax.random.fold_in(key, 11)
    key_values = jax.random.fold_in(key, 0)
    position = jnp.arange(ORDER, dtype=jnp.float32) / ORDER
    row_scale = jnp.exp(0.5 * jnp.log(3.0) * position)
    raw_draw = jax.random.normal(key_values, (ORDER, ORDER), jnp.float32)
    symmetric = (raw_draw + raw_draw.T) * 0.7071
    return 0.15 * symmetric * row_scale[:, None] * row_scale[None, :]


def draw_pattern(key, part):
    key = jax.random.fold_in(key, 23)
    key_shift, key_order = jax.random.split(key)
    offset = jax.random.randint(key_shift, (), 1, NBLK // 2)
    labels = jax.random.permutation(key_order, NBLK)
    row_ids = labels[:, None]
    col_ids = labels[None, :]
    apart = (col_ids - row_ids) % NBLK
    linked = (apart == 0) | (apart == offset) | (apart == NBLK - offset)
    return linked.astype(jnp.int32)


def draw_keep_blocks(key, part):
    key = jax.random.fold_in(key, 37)
    raw_draw = jax.random.randint(key, (NBLK, NBLK), 0, 4)
    row_ids = jnp.arange(NBLK)[:, None]
    col_ids = jnp.arange(NBLK)[None, :]
    kept = (raw_draw > 1).astype(jnp.int32)
    kept = jnp.maximum(kept, kept.T)
    return jnp.maximum(kept, (row_ids == col_ids).astype(jnp.int32)).astype(jnp.int32)


def touch_ends(result, rng, low, largest):
    index_at = [jax.random.randint(jax.random.fold_in(rng, axis), (), 0, length) for axis, length in enumerate(result.shape)]
    widest = result.shape.index(max(result.shape))
    beside = index_at[:widest] + [(index_at[widest] + 1) % result.shape[widest]] + index_at[widest + 1:]
    return result.at[tuple(index_at)].set(low).at[tuple(beside)].set(largest)


def setup_inputs(seed: int = 0, part: int = 0) -> dict:
    key_list = jax.random.split(jax.random.key(seed), 5)
    part_keys = jax.random.split(jax.random.fold_in(key_list[4], part), 5)
    density = draw_density(jax.random.fold_in(jax.random.fold_in(key_list[4], part), 71), part)
    pattern = draw_pattern(jax.random.fold_in(key_list[4], 71), part)
    branch = touch_ends(jax.random.randint(key_list[2], (NBLK,), 0, 2), jax.random.fold_in(key_list[2], 1), 0, 1).astype(jnp.int32)
    keep_blocks = draw_keep_blocks(jax.random.fold_in(key_list[4], 71), part)
    return {"density": density, "pattern": pattern, "branch": branch, "keep_blocks": keep_blocks}


def expand(block_table):
    grown = jnp.repeat(block_table.astype(jnp.float32), BLOCK, axis=0)
    return jnp.repeat(grown, BLOCK, axis=1)


def reference(density, pattern, branch, keep_blocks):
    masked = density * expand(pattern)
    product = jnp.dot(masked, masked, precision=lax.Precision.HIGHEST, preferred_element_type=jnp.float32)
    row_branch = jnp.repeat(branch, BLOCK)
    chosen = jnp.where(row_branch[:, None] == 0, product, 2.0 * masked - product)
    purified = chosen * expand(keep_blocks)
    occupation = (jnp.trace(purified) / ORDER).reshape(1).astype(jnp.float32)
    return purified, occupation
```

```python
import functools

import jax
import jax.numpy as jnp
from jax import lax
from jax.experimental import pallas as pl
from jax.experimental.pallas import tpu as pltpu
from jax.sharding import PartitionSpec as P

BLOCK = 128
HALF = BLOCK // 2
PICKS = 3
MESH = pl.DeviceIdType.MESH


def kernel(
    zsize, ysize, pat, branch, keep, x, out, occ,
    full, mine, buf, sel, bhi, blo, local_sem, ex_sem, send_sem, recv_sem,
):
    n = zsize * ysize
    cols = x.shape[1]
    per = cols // BLOCK
    g = lax.axis_index("grid")
    l = lax.axis_index("layer")
    other = 1 - l
    z = g // ysize
    y = g % ysize

    own_cols = pl.ds(pl.multiple_of(l * cols, BLOCK), cols)
    own_rows = pl.ds(pl.multiple_of(l * HALF, 8), HALF)
    other_rows = pl.ds(pl.multiple_of(other * HALF, 8), HALF)
    load_half = pltpu.make_async_copy(x.at[own_rows, :], full.at[:, own_cols], local_sem.at[0])
    load_half.start()
    load_all = pltpu.make_async_copy(x, mine, local_sem.at[1])
    load_all.start()

    up_ok, down_ok = z + 1 < zsize, z > 0
    up, down = (z + 1) * ysize + y, (z - 1) * ysize + y
    across = z * ysize + (1 - y)

    barrier = pltpu.get_barrier_semaphore()
    pl.semaphore_signal(barrier, inc=1, device_id={"layer": other}, device_id_type=MESH)
    if ysize == 2:
        pl.semaphore_signal(barrier, inc=1, device_id={"grid": across}, device_id_type=MESH)

    @pl.when(up_ok)
    def _():
        pl.semaphore_signal(barrier, inc=1, device_id={"grid": up}, device_id_type=MESH)

    @pl.when(down_ok)
    def _():
        pl.semaphore_signal(barrier, inc=1, device_id={"grid": down}, device_id_type=MESH)

    peers = ysize + up_ok.astype(jnp.int32) + down_ok.astype(jnp.int32)
    pl.semaphore_wait(barrier, peers)

    exchange = pltpu.make_async_remote_copy(
        src_ref=x.at[other_rows, :], dst_ref=full.at[:, own_cols],
        send_sem=ex_sem.at[0], recv_sem=ex_sem.at[1],
        device_id={"layer": other}, device_id_type=MESH,
    )
    exchange.start()

    def picks(row):
        count = jnp.int32(0)
        found = [jnp.int32(0)] * PICKS
        for j in range(n):
            here = pat[row, j]
            for s in range(PICKS):
                found[s] = jnp.where((here == 1) & (count == s), j, found[s])
            count = count + here
        return found

    near = picks(g)
    flag = branch[g]
    zero = jnp.int32(0)
    link = []
    for s in range(PICKS):
        link.append([
            sum((jnp.where(near[s] == j, pat[j, c], zero) for j in range(n)), zero)
            for c in range(n)
        ])
    sel[...] = jnp.zeros(sel.shape, jnp.float32)

    def choose(h, gp):
        for s in range(PICKS):
            piece = buf[h, gp, :PICKS * HALF, :]
            sel[s, h] = jnp.where(near[s] == gp, piece, sel[s, h])

    def piece_copy(way, target, gp):
        return pltpu.make_async_remote_copy(
            src_ref=buf.at[l, gp], dst_ref=buf.at[l, gp],
            send_sem=send_sem.at[way, gp], recv_sem=recv_sem.at[l, gp],
            device_id=target, device_id_type=MESH,
        )

    def to_up(gp):
        return piece_copy(0, {"grid": up}, gp)

    def to_down(gp):
        return piece_copy(1, {"grid": down}, gp)

    def to_across(gp):
        return piece_copy(2, {"grid": across}, gp)

    def to_core(gp):
        return piece_copy(3, {"layer": other}, gp)

    def arrived(h, gp):
        pltpu.make_async_remote_copy(
            src_ref=buf.at[h, gp], dst_ref=buf.at[h, gp],
            send_sem=send_sem.at[3, gp], recv_sem=recv_sem.at[h, gp],
            device_id={"layer": other}, device_id_type=MESH,
        ).wait_recv()

    load_half.wait()
    exchange.wait()

    squares = jnp.zeros((8, BLOCK), jnp.float32)
    for s in range(PICKS):
        block = jnp.zeros((HALF, BLOCK), jnp.float32)
        for j in range(n):
            block = jnp.where(near[s] == j, full[:, j * BLOCK:(j + 1) * BLOCK], block)
        buf[l, g, s * HALF:(s + 1) * HALF, :] = block
        squares = squares + jnp.sum((block * block).reshape(HALF // 8, 8, BLOCK), axis=0)
    diagonal = full[:, pl.ds(pl.multiple_of(g * BLOCK, BLOCK), BLOCK)]
    at_row = lax.broadcasted_iota(jnp.int32, (HALF, BLOCK), 0) + l * HALF
    at_col = lax.broadcasted_iota(jnp.int32, (HALF, BLOCK), 1)
    diagonal = jnp.where(at_row == at_col, diagonal, 0.0)
    twice = 2.0 * jnp.sum(diagonal.reshape(HALF // 8, 8, BLOCK), axis=0)
    buf[l, g, PICKS * HALF:, :] = jnp.where(flag == 1, twice - squares, squares)

    @pl.when(up_ok)
    def _():
        to_up(g).start()

    @pl.when(down_ok)
    def _():
        to_down(g).start()

    if ysize == 2:
        to_across(g).start()
    to_core(g).start()
    choose(l, g)

    def column(d, yy, act):
        def at(zz):
            act(zz * ysize + yy)

        if d == 0:
            at(z)
            return

        @pl.when(z - d >= 0)
        def _():
            at(z - d)

        @pl.when(z + d < zsize)
        def _():
            at(z + d)

    def across_arrives(gp):
        arrived(l, gp)
        to_core(gp).start()
        choose(l, gp)

    def core_arrives(gp):
        arrived(other, gp)
        choose(other, gp)

    for d in range(1, zsize + 1):
        if d < zsize:
            @pl.when(z - d >= 0)
            def _(d=d):
                gp = (z - d) * ysize + y
                arrived(l, gp)

                @pl.when(up_ok)
                def _():
                    to_up(gp).start()

                if ysize == 2:
                    to_across(gp).start()
                to_core(gp).start()
                choose(l, gp)

            @pl.when(z + d < zsize)
            def _(d=d):
                gp = (z + d) * ysize + y
                arrived(l, gp)

                @pl.when(down_ok)
                def _():
                    to_down(gp).start()

                if ysize == 2:
                    to_across(gp).start()
                to_core(gp).start()
                choose(l, gp)

        if ysize == 2:
            column(d - 1, 1 - y, across_arrives)
        column(d - 1, y, core_arrives)
        if ysize == 2 and d > 1:
            column(d - 2, 1 - y, core_arrives)
    if ysize == 2:
        column(zsize - 1, 1 - y, core_arrives)
    load_all.wait()

    total = jnp.zeros((8, BLOCK), jnp.float32)
    for gp in range(n):
        for h in range(2):
            total = total + buf[h, gp, PICKS * HALF:, :]
    occ[0] = jnp.sum(total) * (1.0 / (n * BLOCK))

    def split(value):
        high = value.astype(jnp.bfloat16)
        return high, (value - high.astype(jnp.float32)).astype(jnp.bfloat16)

    for s in range(PICKS):
        count = zero
        counts = []
        for c in range(n):
            counts.append(count)
            count = count + link[s][c]
        for c in range(per):
            here = jnp.where(l == 0, link[s][c], link[s][per + c])
            slot = jnp.where(l == 0, counts[c], counts[per + c])
            slot = jnp.where(here == 1, slot, PICKS)
            for h in range(2):
                block = jnp.zeros((HALF, BLOCK), jnp.float32)
                for q in range(PICKS):
                    block = jnp.where(slot == q, sel[s, h, q * HALF:(q + 1) * HALF, :], block)
                high, low = split(block)
                rows = slice(s * BLOCK + h * HALF, s * BLOCK + (h + 1) * HALF)
                bhi[rows, c * BLOCK:(c + 1) * BLOCK] = high
                blo[rows, c * BLOCK:(c + 1) * BLOCK] = low

    ahi, alo = [], []
    for s in range(PICKS):
        block = jnp.concatenate(
            [buf[h, g, s * HALF:(s + 1) * HALF, :] for h in range(2)], axis=0
        )
        high, low = split(block)
        ahi.append(high)
        alo.append(low)
    ahi = jnp.concatenate(ahi, axis=1)
    alo = jnp.concatenate(alo, axis=1)
    dot = functools.partial(jnp.dot, preferred_element_type=jnp.float32)
    wide = min(cols, 512)
    for w in range(cols // wide):
        span = slice(w * wide, (w + 1) * wide)
        high, low = bhi[:, span], blo[:, span]
        product = dot(ahi, high) + (dot(ahi, low) + dot(alo, high))
        for i in range(wide // BLOCK):
            c = w * (wide // BLOCK) + i
            col = slice(c * BLOCK, (c + 1) * BLOCK)
            part = product[:, i * BLOCK:(i + 1) * BLOCK]
            masked = jnp.where(pat[g, l * per + c] == 1, mine[:, col], 0.0)
            chosen = jnp.where(flag == 1, 2.0 * masked - part, part)
            out[:, col] = jnp.where(keep[g, l * per + c] == 1, chosen, 0.0)

    if ysize == 2:
        to_across(g).wait_send()
    for gp in range(n):
        zz, yy = gp // ysize, gp % ysize
        to_core(gp).wait_send()

        @pl.when((yy == y) & (zz <= z) & up_ok)
        def _(gp=gp):
            to_up(gp).wait_send()

        @pl.when((yy == y) & (zz >= z) & down_ok)
        def _(gp=gp):
            to_down(gp).wait_send()

        if ysize == 2:
            @pl.when((yy == y) & (zz != z))
            def _(gp=gp):
                to_across(gp).wait_send()


def shards(zsize, ysize, density, pattern, branch, keep_blocks):
    rows, cols = density.shape
    n = zsize * ysize
    smem = pl.BlockSpec(memory_space=pltpu.SMEM)
    return pl.pallas_call(
        functools.partial(kernel, zsize, ysize),
        out_shape=(
            jax.ShapeDtypeStruct((rows, cols), jnp.float32),
            jax.ShapeDtypeStruct((1,), jnp.float32),
        ),
        in_specs=[smem, smem, smem, pl.BlockSpec(memory_space=pl.ANY)],
        out_specs=(pl.BlockSpec(memory_space=pltpu.VMEM), smem),
        scratch_shapes=[
            pltpu.VMEM((HALF, 2 * cols), jnp.float32),
            pltpu.VMEM((rows, cols), jnp.float32),
            pltpu.VMEM((2, n, PICKS * HALF + 8, BLOCK), jnp.float32),
            pltpu.VMEM((PICKS, 2, PICKS * HALF, BLOCK), jnp.float32),
            pltpu.VMEM((PICKS * BLOCK, cols), jnp.bfloat16),
            pltpu.VMEM((PICKS * BLOCK, cols), jnp.bfloat16),
            pltpu.SemaphoreType.DMA((2,)),
            pltpu.SemaphoreType.DMA((2,)),
            pltpu.SemaphoreType.DMA((4, n)),
            pltpu.SemaphoreType.DMA((2, n)),
        ],
        compiler_params=pltpu.CompilerParams(
            collective_id=0, has_side_effects=True, vmem_limit_bytes=40 * 1024 * 1024
        ),
        name="sp2",
    )(pattern, branch, keep_blocks, density)


def solution(mesh):
    n = mesh.shape["grid"]
    ysize = 2 if n == 8 else 1
    placed = (P(("groups", "grid"), "layer"), P(), P(), P())
    return jax.shard_map(
        functools.partial(shards, n // ysize, ysize),
        mesh=mesh,
        in_specs=placed,
        out_specs=(P(("groups", "grid"), "layer"), P("groups")),
        check_vma=False,
    )
```

```python
import functools

import jax
import jax.numpy as jnp
from jax import lax
from jax.experimental import pallas as pl
from jax.experimental.pallas import tpu as pltpu
from jax.sharding import PartitionSpec as P

BLOCK = 128
HALF = BLOCK // 2
PICKS = 3
CHUNKS = (slice(0, 96), slice(96, PICKS * HALF + 8))
MESH = pl.DeviceIdType.MESH


def kernel(
    zsize, ysize, pat_in, branch_in, keep_in, x, out, occ,
    pat, branch, keep,
    full, mine, buf, sel, bhi, blo, local_sem, ex_sem, send_sem, recv_sem,
):
    n = zsize * ysize
    cols = x.shape[1]
    per = cols // BLOCK
    g = lax.axis_index("grid")
    l = lax.axis_index("layer")
    other = 1 - l
    z = g // ysize
    y = g % ysize

    own_cols = pl.ds(pl.multiple_of(l * cols, BLOCK), cols)
    own_rows = pl.ds(pl.multiple_of(l * HALF, 8), HALF)
    other_rows = pl.ds(pl.multiple_of(other * HALF, 8), HALF)
    load_half = pltpu.make_async_copy(x.at[own_rows, :], full.at[:, own_cols], local_sem.at[0])
    load_half.start()
    load_all = pltpu.make_async_copy(x, mine, local_sem.at[1])
    load_all.start()

    tables = [
        pltpu.make_async_copy(source, held, local_sem.at[2 + i])
        for i, (source, held) in enumerate(((pat_in, pat), (branch_in, branch), (keep_in, keep)))
    ]
    for table in tables:
        table.start()

    up_ok, down_ok = z + 1 < zsize, z > 0
    up, down = (z + 1) * ysize + y, (z - 1) * ysize + y
    across = z * ysize + (1 - y)

    barrier = pltpu.get_barrier_semaphore()
    pl.semaphore_signal(barrier, inc=1, device_id={"layer": other}, device_id_type=MESH)
    if ysize == 2:
        pl.semaphore_signal(barrier, inc=1, device_id={"grid": across}, device_id_type=MESH)

    @pl.when(up_ok)
    def _():
        pl.semaphore_signal(barrier, inc=1, device_id={"grid": up}, device_id_type=MESH)

    @pl.when(down_ok)
    def _():
        pl.semaphore_signal(barrier, inc=1, device_id={"grid": down}, device_id_type=MESH)

    peers = ysize + up_ok.astype(jnp.int32) + down_ok.astype(jnp.int32)
    pl.semaphore_wait(barrier, peers)

    exchange = pltpu.make_async_remote_copy(
        src_ref=x.at[other_rows, :], dst_ref=full.at[:, own_cols],
        send_sem=ex_sem.at[0], recv_sem=ex_sem.at[1],
        device_id={"layer": other}, device_id_type=MESH,
    )
    exchange.start()

    def picks(row):
        count = jnp.int32(0)
        found = [jnp.int32(0)] * PICKS
        for j in range(n):
            here = pat[row, j]
            for s in range(PICKS):
                found[s] = jnp.where((here == 1) & (count == s), j, found[s])
            count = count + here
        return found

    for table in tables:
        table.wait()
    near = picks(g)
    flag = branch[g]
    zero = jnp.int32(0)
    link = []
    for s in range(PICKS):
        link.append([
            sum((jnp.where(near[s] == j, pat[j, c], zero) for j in range(n)), zero)
            for c in range(n)
        ])
    sel[...] = jnp.zeros(sel.shape, jnp.float32)

    def choose(h, gp):
        for s in range(PICKS):
            piece = buf[h, gp, :PICKS * HALF, :]
            sel[s, h] = jnp.where(near[s] == gp, piece, sel[s, h])

    def piece_copy(way, target, h, gp, q):
        return pltpu.make_async_remote_copy(
            src_ref=buf.at[h, gp, CHUNKS[q]], dst_ref=buf.at[h, gp, CHUNKS[q]],
            send_sem=send_sem.at[way, gp, q], recv_sem=recv_sem.at[h, gp, q],
            device_id=target, device_id_type=MESH,
        )

    def to_up(gp, q):
        return piece_copy(0, {"grid": up}, l, gp, q)

    def to_down(gp, q):
        return piece_copy(1, {"grid": down}, l, gp, q)

    def to_across(gp, q):
        return piece_copy(2, {"grid": across}, l, gp, q)

    def to_core(gp, q):
        return piece_copy(3, {"layer": other}, l, gp, q)

    def arrived(h, gp, q):
        piece_copy(3, {"layer": other}, h, gp, q).wait_recv()

    load_half.wait()
    exchange.wait()

    squares = jnp.zeros((8, BLOCK), jnp.float32)
    for s in range(PICKS):
        block = jnp.zeros((HALF, BLOCK), jnp.float32)
        for j in range(n):
            block = jnp.where(near[s] == j, full[:, j * BLOCK:(j + 1) * BLOCK], block)
        buf[l, g, s * HALF:(s + 1) * HALF, :] = block
        squares = squares + jnp.sum((block * block).reshape(HALF // 8, 8, BLOCK), axis=0)
    diagonal = full[:, pl.ds(pl.multiple_of(g * BLOCK, BLOCK), BLOCK)]
    at_row = lax.broadcasted_iota(jnp.int32, (HALF, BLOCK), 0) + l * HALF
    at_col = lax.broadcasted_iota(jnp.int32, (HALF, BLOCK), 1)
    diagonal = jnp.where(at_row == at_col, diagonal, 0.0)
    twice = 2.0 * jnp.sum(diagonal.reshape(HALF // 8, 8, BLOCK), axis=0)
    buf[l, g, PICKS * HALF:, :] = jnp.where(flag == 1, twice - squares, squares)

    for q in range(len(CHUNKS)):
        @pl.when(up_ok)
        def _(q=q):
            to_up(g, q).start()

        @pl.when(down_ok)
        def _(q=q):
            to_down(g, q).start()

        if ysize == 2:
            to_across(g, q).start()
        to_core(g, q).start()
    choose(l, g)

    def column(d, yy, act):
        def at(zz):
            act(zz * ysize + yy)

        if d == 0:
            at(z)
            return

        @pl.when(z - d >= 0)
        def _():
            at(z - d)

        @pl.when(z + d < zsize)
        def _():
            at(z + d)

    def across_arrives(gp):
        for q in range(len(CHUNKS)):
            arrived(l, gp, q)
            to_core(gp, q).start()
        choose(l, gp)

    def core_arrives(gp):
        for q in range(len(CHUNKS)):
            arrived(other, gp, q)
        choose(other, gp)

    def pass_on(gp, q, further, way):
        arrived(l, gp, q)

        @pl.when(further)
        def _():
            way(gp, q).start()

        if ysize == 2:
            to_across(gp, q).start()
        to_core(gp, q).start()

    for d in range(1, zsize + 1):
        if d < zsize:
            for q in range(len(CHUNKS)):
                @pl.when(z - d >= 0)
                def _(d=d, q=q):
                    pass_on((z - d) * ysize + y, q, up_ok, to_up)

                @pl.when(z + d < zsize)
                def _(d=d, q=q):
                    pass_on((z + d) * ysize + y, q, down_ok, to_down)

            column(d, y, functools.partial(choose, l))

        if ysize == 2:
            column(d - 1, 1 - y, across_arrives)
        column(d - 1, y, core_arrives)
        if ysize == 2 and d > 1:
            column(d - 2, 1 - y, core_arrives)
    if ysize == 2:
        column(zsize - 1, 1 - y, core_arrives)
    load_all.wait()

    total = jnp.zeros((8, BLOCK), jnp.float32)
    for gp in range(n):
        for h in range(2):
            total = total + buf[h, gp, PICKS * HALF:, :]
    occ[0] = jnp.sum(total) * (1.0 / (n * BLOCK))

    def split(value):
        high = value.astype(jnp.bfloat16)
        return high, (value - high.astype(jnp.float32)).astype(jnp.bfloat16)

    for s in range(PICKS):
        count = zero
        counts = []
        for c in range(n):
            counts.append(count)
            count = count + link[s][c]
        for c in range(per):
            here = jnp.where(l == 0, link[s][c], link[s][per + c])
            slot = jnp.where(l == 0, counts[c], counts[per + c])
            slot = jnp.where(here == 1, slot, PICKS)
            for h in range(2):
                block = jnp.zeros((HALF, BLOCK), jnp.float32)
                for q in range(PICKS):
                    block = jnp.where(slot == q, sel[s, h, q * HALF:(q + 1) * HALF, :], block)
                high, low = split(block)
                rows = slice(s * BLOCK + h * HALF, s * BLOCK + (h + 1) * HALF)
                bhi[rows, c * BLOCK:(c + 1) * BLOCK] = high
                blo[rows, c * BLOCK:(c + 1) * BLOCK] = low

    ahi, alo = [], []
    for s in range(PICKS):
        block = jnp.concatenate(
            [buf[h, g, s * HALF:(s + 1) * HALF, :] for h in range(2)], axis=0
        )
        high, low = split(block)
        ahi.append(high)
        alo.append(low)
    ahi = jnp.concatenate(ahi, axis=1)
    alo = jnp.concatenate(alo, axis=1)
    dot = functools.partial(jnp.dot, preferred_element_type=jnp.float32)
    wide = min(cols, 512)
    for w in range(cols // wide):
        span = slice(w * wide, (w + 1) * wide)
        high, low = bhi[:, span], blo[:, span]
        product = dot(ahi, high) + (dot(ahi, low) + dot(alo, high))
        for i in range(wide // BLOCK):
            c = w * (wide // BLOCK) + i
            col = slice(c * BLOCK, (c + 1) * BLOCK)
            part = product[:, i * BLOCK:(i + 1) * BLOCK]
            masked = jnp.where(pat[g, l * per + c] == 1, mine[:, col], 0.0)
            chosen = jnp.where(flag == 1, 2.0 * masked - part, part)
            out[:, col] = jnp.where(keep[g, l * per + c] == 1, chosen, 0.0)

    for gp in range(n):
        zz, yy = gp // ysize, gp % ysize
        for q in range(len(CHUNKS)):
            to_core(gp, q).wait_send()

            @pl.when((yy == y) & (zz <= z) & up_ok)
            def _(gp=gp, q=q):
                to_up(gp, q).wait_send()

            @pl.when((yy == y) & (zz >= z) & down_ok)
            def _(gp=gp, q=q):
                to_down(gp, q).wait_send()

            if ysize == 2:
                @pl.when(yy == y)
                def _(gp=gp, q=q):
                    to_across(gp, q).wait_send()


def shards(zsize, ysize, density, pattern, branch, keep_blocks):
    rows, cols = density.shape
    n = zsize * ysize
    smem = pl.BlockSpec(memory_space=pltpu.SMEM)
    return pl.pallas_call(
        functools.partial(kernel, zsize, ysize),
        out_shape=(
            jax.ShapeDtypeStruct((rows, cols), jnp.float32),
            jax.ShapeDtypeStruct((1,), jnp.float32),
        ),
        in_specs=[pl.BlockSpec(memory_space=pltpu.HBM)] * 4,
        out_specs=(pl.BlockSpec(memory_space=pltpu.VMEM), smem),
        scratch_shapes=[
            pltpu.SMEM(pattern.shape, jnp.int32),
            pltpu.SMEM(branch.shape, jnp.int32),
            pltpu.SMEM(keep_blocks.shape, jnp.int32),
            pltpu.VMEM((HALF, 2 * cols), jnp.float32),
            pltpu.VMEM((rows, cols), jnp.float32),
            pltpu.VMEM((2, n, PICKS * HALF + 8, BLOCK), jnp.float32),
            pltpu.VMEM((PICKS, 2, PICKS * HALF, BLOCK), jnp.float32),
            pltpu.VMEM((PICKS * BLOCK, cols), jnp.bfloat16),
            pltpu.VMEM((PICKS * BLOCK, cols), jnp.bfloat16),
            pltpu.SemaphoreType.DMA((5,)),
            pltpu.SemaphoreType.DMA((2,)),
            pltpu.SemaphoreType.DMA((4, n, len(CHUNKS))),
            pltpu.SemaphoreType.DMA((2, n, len(CHUNKS))),
        ],
        compiler_params=pltpu.CompilerParams(
            collective_id=0, has_side_effects=True, vmem_limit_bytes=60 * 1024 * 1024
        ),
        name="sp2",
    )(pattern, branch, keep_blocks, density)


def solution(mesh):
    n = mesh.shape["grid"]
    ysize = 2 if n == 8 else 1
    placed = (P(("groups", "grid"), "layer"), P(), P(), P())
    return jax.shard_map(
        functools.partial(shards, n // ysize, ysize),
        mesh=mesh,
        in_specs=placed,
        out_specs=(P(("groups", "grid"), "layer"), P("groups")),
        check_vma=False,
    )
```

```python
import functools

import jax
import jax.numpy as jnp
from jax import lax
from jax.experimental import pallas as pl
from jax.experimental.pallas import tpu as pltpu
from jax.sharding import PartitionSpec as P

BLOCK = 128
HALF = BLOCK // 2
PICKS = 3
CHUNKS = (slice(0, 96), slice(96, PICKS * HALF + 8))
MESH = pl.DeviceIdType.MESH


def kernel(
    zsize, ysize, pat_in, branch_in, keep_in, x, out, occ,
    pat, branch, keep,
    full, mine, buf, sel, bhi, blo, local_sem, ex_sem, send_sem, recv_sem,
):
    n = zsize * ysize
    cols = x.shape[1]
    per = cols // BLOCK
    g = lax.axis_index("grid")
    l = lax.axis_index("layer")
    other = 1 - l
    z = g // ysize
    y = g % ysize

    own_cols = pl.ds(pl.multiple_of(l * cols, BLOCK), cols)
    own_rows = pl.ds(pl.multiple_of(l * HALF, 8), HALF)
    other_rows = pl.ds(pl.multiple_of(other * HALF, 8), HALF)
    load_half = pltpu.make_async_copy(x.at[own_rows, :], full.at[:, own_cols], local_sem.at[0])
    load_half.start()
    load_all = pltpu.make_async_copy(x, mine, local_sem.at[1])
    load_all.start()

    tables = [
        pltpu.make_async_copy(source, held, local_sem.at[2 + i])
        for i, (source, held) in enumerate(((pat_in, pat), (branch_in, branch), (keep_in, keep)))
    ]
    for table in tables:
        table.start()

    up_ok, down_ok = z + 1 < zsize, z > 0
    up, down = (z + 1) * ysize + y, (z - 1) * ysize + y
    across = z * ysize + (1 - y)

    barrier = pltpu.get_barrier_semaphore()
    pl.semaphore_signal(barrier, inc=1, device_id={"layer": other}, device_id_type=MESH)
    if ysize == 2:
        pl.semaphore_signal(barrier, inc=1, device_id={"grid": across}, device_id_type=MESH)

    @pl.when(up_ok)
    def _():
        pl.semaphore_signal(barrier, inc=1, device_id={"grid": up}, device_id_type=MESH)

    @pl.when(down_ok)
    def _():
        pl.semaphore_signal(barrier, inc=1, device_id={"grid": down}, device_id_type=MESH)

    peers = ysize + up_ok.astype(jnp.int32) + down_ok.astype(jnp.int32)
    pl.semaphore_wait(barrier, peers)

    exchange = pltpu.make_async_remote_copy(
        src_ref=x.at[other_rows, :], dst_ref=full.at[:, own_cols],
        send_sem=ex_sem.at[0], recv_sem=ex_sem.at[1],
        device_id={"layer": other}, device_id_type=MESH,
    )
    exchange.start()

    def picks(row):
        count = jnp.int32(0)
        found = [jnp.int32(0)] * PICKS
        for j in range(n):
            here = pat[row, j]
            for s in range(PICKS):
                found[s] = jnp.where((here == 1) & (count == s), j, found[s])
            count = count + here
        return found

    for table in tables:
        table.wait()
    near = picks(g)
    flag = branch[g]
    def choose(h, gp):
        for s in range(PICKS):
            piece = buf[h, gp, :PICKS * HALF, :]
            sel[s, h] = jnp.where(near[s] == gp, piece, sel[s, h])

    def piece_copy(way, target, h, gp, q):
        return pltpu.make_async_remote_copy(
            src_ref=buf.at[h, gp, CHUNKS[q]], dst_ref=buf.at[h, gp, CHUNKS[q]],
            send_sem=send_sem.at[way, gp, q], recv_sem=recv_sem.at[h, gp, q],
            device_id=target, device_id_type=MESH,
        )

    def to_up(gp, q):
        return piece_copy(0, {"grid": up}, l, gp, q)

    def to_down(gp, q):
        return piece_copy(1, {"grid": down}, l, gp, q)

    def to_across(gp, q):
        return piece_copy(2, {"grid": across}, l, gp, q)

    def to_core(gp, q):
        return piece_copy(3, {"layer": other}, l, gp, q)

    def arrived(h, gp, q):
        piece_copy(3, {"layer": other}, h, gp, q).wait_recv()

    load_half.wait()
    exchange.wait()

    squares = jnp.zeros((8, BLOCK), jnp.float32)
    for s in range(PICKS):
        block = jnp.zeros((HALF, BLOCK), jnp.float32)
        for j in range(n):
            block = jnp.where(near[s] == j, full[:, j * BLOCK:(j + 1) * BLOCK], block)
        buf[l, g, s * HALF:(s + 1) * HALF, :] = block
        squares = squares + jnp.sum((block * block).reshape(HALF // 8, 8, BLOCK), axis=0)
    diagonal = full[:, pl.ds(pl.multiple_of(g * BLOCK, BLOCK), BLOCK)]
    at_row = lax.broadcasted_iota(jnp.int32, (HALF, BLOCK), 0) + l * HALF
    at_col = lax.broadcasted_iota(jnp.int32, (HALF, BLOCK), 1)
    diagonal = jnp.where(at_row == at_col, diagonal, 0.0)
    twice = 2.0 * jnp.sum(diagonal.reshape(HALF // 8, 8, BLOCK), axis=0)
    buf[l, g, PICKS * HALF:, :] = jnp.where(flag == 1, twice - squares, squares)

    for q in range(len(CHUNKS)):
        @pl.when(up_ok)
        def _(q=q):
            to_up(g, q).start()

        @pl.when(down_ok)
        def _(q=q):
            to_down(g, q).start()

        if ysize == 2:
            to_across(g, q).start()
        to_core(g, q).start()
    zero = jnp.int32(0)
    link = []
    for s in range(PICKS):
        link.append([
            sum((jnp.where(near[s] == j, pat[j, c], zero) for j in range(n)), zero)
            for c in range(n)
        ])
    sel[...] = jnp.zeros(sel.shape, jnp.float32)

    choose(l, g)

    def column(d, yy, act):
        def at(zz):
            act(zz * ysize + yy)

        if d == 0:
            at(z)
            return

        @pl.when(z - d >= 0)
        def _():
            at(z - d)

        @pl.when(z + d < zsize)
        def _():
            at(z + d)

    def across_arrives(gp):
        for q in range(len(CHUNKS)):
            arrived(l, gp, q)
            to_core(gp, q).start()
        choose(l, gp)

    def core_arrives(gp):
        for q in range(len(CHUNKS)):
            arrived(other, gp, q)
        choose(other, gp)

    def pass_on(gp, q, further, way):
        arrived(l, gp, q)

        @pl.when(further)
        def _():
            way(gp, q).start()

        if ysize == 2:
            to_across(gp, q).start()
        to_core(gp, q).start()

    for d in range(1, zsize + 1):
        if d < zsize:
            for q in range(len(CHUNKS)):
                @pl.when(z - d >= 0)
                def _(d=d, q=q):
                    pass_on((z - d) * ysize + y, q, up_ok, to_up)

                @pl.when(z + d < zsize)
                def _(d=d, q=q):
                    pass_on((z + d) * ysize + y, q, down_ok, to_down)

            column(d, y, functools.partial(choose, l))

        if ysize == 2:
            column(d - 1, 1 - y, across_arrives)
        column(d - 1, y, core_arrives)
        if ysize == 2 and d > 1:
            column(d - 2, 1 - y, core_arrives)
    if ysize == 2:
        column(zsize - 1, 1 - y, core_arrives)
    load_all.wait()

    total = jnp.zeros((8, BLOCK), jnp.float32)
    for gp in range(n):
        for h in range(2):
            total = total + buf[h, gp, PICKS * HALF:, :]
    occ[0] = jnp.sum(total) * (1.0 / (n * BLOCK))

    def split(value):
        high = value.astype(jnp.bfloat16)
        return high, (value - high.astype(jnp.float32)).astype(jnp.bfloat16)

    for s in range(PICKS):
        count = zero
        counts = []
        for c in range(n):
            counts.append(count)
            count = count + link[s][c]
        for c in range(per):
            here = jnp.where(l == 0, link[s][c], link[s][per + c])
            slot = jnp.where(l == 0, counts[c], counts[per + c])
            slot = jnp.where(here == 1, slot, PICKS)
            for h in range(2):
                block = jnp.zeros((HALF, BLOCK), jnp.float32)
                for q in range(PICKS):
                    block = jnp.where(slot == q, sel[s, h, q * HALF:(q + 1) * HALF, :], block)
                high, low = split(block)
                rows = slice(s * BLOCK + h * HALF, s * BLOCK + (h + 1) * HALF)
                bhi[rows, c * BLOCK:(c + 1) * BLOCK] = high
                blo[rows, c * BLOCK:(c + 1) * BLOCK] = low

    ahi, alo = [], []
    for s in range(PICKS):
        block = jnp.concatenate(
            [buf[h, g, s * HALF:(s + 1) * HALF, :] for h in range(2)], axis=0
        )
        high, low = split(block)
        ahi.append(high)
        alo.append(low)
    ahi = jnp.concatenate(ahi, axis=1)
    alo = jnp.concatenate(alo, axis=1)
    dot = functools.partial(jnp.dot, preferred_element_type=jnp.float32)
    wide = min(cols, 512)
    for w in range(cols // wide):
        span = slice(w * wide, (w + 1) * wide)
        high, low = bhi[:, span], blo[:, span]
        product = dot(ahi, high) + (dot(ahi, low) + dot(alo, high))
        for i in range(wide // BLOCK):
            c = w * (wide // BLOCK) + i
            col = slice(c * BLOCK, (c + 1) * BLOCK)
            part = product[:, i * BLOCK:(i + 1) * BLOCK]
            masked = jnp.where(pat[g, l * per + c] == 1, mine[:, col], 0.0)
            chosen = jnp.where(flag == 1, 2.0 * masked - part, part)
            out[:, col] = jnp.where(keep[g, l * per + c] == 1, chosen, 0.0)

    for gp in range(n):
        zz, yy = gp // ysize, gp % ysize
        for q in range(len(CHUNKS)):
            to_core(gp, q).wait_send()

            @pl.when((yy == y) & (zz <= z) & up_ok)
            def _(gp=gp, q=q):
                to_up(gp, q).wait_send()

            @pl.when((yy == y) & (zz >= z) & down_ok)
            def _(gp=gp, q=q):
                to_down(gp, q).wait_send()

            if ysize == 2:
                @pl.when(yy == y)
                def _(gp=gp, q=q):
                    to_across(gp, q).wait_send()


def shards(zsize, ysize, density, pattern, branch, keep_blocks):
    rows, cols = density.shape
    n = zsize * ysize
    smem = pl.BlockSpec(memory_space=pltpu.SMEM)
    return pl.pallas_call(
        functools.partial(kernel, zsize, ysize),
        out_shape=(
            pltpu.VMEM((rows, cols), jnp.float32),
            jax.ShapeDtypeStruct((1,), jnp.float32),
        ),
        in_specs=[pl.BlockSpec(memory_space=pltpu.HBM)] * 4,
        out_specs=(pl.BlockSpec(memory_space=pltpu.VMEM), smem),
        scratch_shapes=[
            pltpu.SMEM(pattern.shape, jnp.int32),
            pltpu.SMEM(branch.shape, jnp.int32),
            pltpu.SMEM(keep_blocks.shape, jnp.int32),
            pltpu.VMEM((HALF, 2 * cols), jnp.float32),
            pltpu.VMEM((rows, cols), jnp.float32),
            pltpu.VMEM((2, n, PICKS * HALF + 8, BLOCK), jnp.float32),
            pltpu.VMEM((PICKS, 2, PICKS * HALF, BLOCK), jnp.float32),
            pltpu.VMEM((PICKS * BLOCK, cols), jnp.bfloat16),
            pltpu.VMEM((PICKS * BLOCK, cols), jnp.bfloat16),
            pltpu.SemaphoreType.DMA((5,)),
            pltpu.SemaphoreType.DMA((2,)),
            pltpu.SemaphoreType.DMA((4, n, len(CHUNKS))),
            pltpu.SemaphoreType.DMA((2, n, len(CHUNKS))),
        ],
        compiler_params=pltpu.CompilerParams(
            collective_id=0, has_side_effects=True, vmem_limit_bytes=40 * 1024 * 1024
        ),
        name="sp2",
    )(*(pltpu.with_memory_space_constraint(v, pltpu.HBM) for v in (pattern, branch, keep_blocks, density)))


def solution(mesh):
    n = mesh.shape["grid"]
    ysize = 2 if n == 8 else 1
    placed = (P(("groups", "grid"), "layer"), P(), P(), P())
    return jax.shard_map(
        functools.partial(shards, n // ysize, ysize),
        mesh=mesh,
        in_specs=placed,
        out_specs=(P(("groups", "grid"), "layer"), P("groups")),
        check_vma=False,
    )
```

```python
import functools

import jax
import jax.numpy as jnp
from jax import lax
from jax.experimental import pallas as pl
from jax.experimental.pallas import tpu as pltpu
from jax.sharding import PartitionSpec as P

BLOCK = 128
HALF = BLOCK // 2
PICKS = 3
CHUNKS = (slice(0, HALF), slice(HALF, 2 * HALF), slice(2 * HALF, PICKS * HALF + 8))
MESH = pl.DeviceIdType.MESH


def kernel(
    zsize, ysize, pat_in, branch_in, keep_in, x, out, occ,
    pat, branch, keep,
    full, mine, buf, sel, bhi, blo, local_sem, ex_sem, send_sem, recv_sem,
):
    n = zsize * ysize
    cols = x.shape[1]
    per = cols // BLOCK
    g = lax.axis_index("grid")
    l = lax.axis_index("layer")
    other = 1 - l
    z = g // ysize
    y = g % ysize

    own_cols = pl.ds(pl.multiple_of(l * cols, BLOCK), cols)
    own_rows = pl.ds(pl.multiple_of(l * HALF, 8), HALF)
    other_rows = pl.ds(pl.multiple_of(other * HALF, 8), HALF)
    load_half = pltpu.make_async_copy(x.at[own_rows, :], full.at[:, own_cols], local_sem.at[0])
    load_half.start()
    load_all = pltpu.make_async_copy(x, mine, local_sem.at[1])
    load_all.start()

    tables = [
        pltpu.make_async_copy(source, held, local_sem.at[2 + i])
        for i, (source, held) in enumerate(((pat_in, pat), (branch_in, branch), (keep_in, keep)))
    ]
    for table in tables:
        table.start()

    up_ok, down_ok = z + 1 < zsize, z > 0
    up, down = (z + 1) * ysize + y, (z - 1) * ysize + y
    across = z * ysize + (1 - y)

    barrier = pltpu.get_barrier_semaphore()
    pl.semaphore_signal(barrier, inc=1, device_id={"layer": other}, device_id_type=MESH)
    if ysize == 2:
        pl.semaphore_signal(barrier, inc=1, device_id={"grid": across}, device_id_type=MESH)

    @pl.when(up_ok)
    def _():
        pl.semaphore_signal(barrier, inc=1, device_id={"grid": up}, device_id_type=MESH)

    @pl.when(down_ok)
    def _():
        pl.semaphore_signal(barrier, inc=1, device_id={"grid": down}, device_id_type=MESH)

    peers = ysize + up_ok.astype(jnp.int32) + down_ok.astype(jnp.int32)
    pl.semaphore_wait(barrier, peers)

    exchange = pltpu.make_async_remote_copy(
        src_ref=x.at[other_rows, :], dst_ref=full.at[:, own_cols],
        send_sem=ex_sem.at[0], recv_sem=ex_sem.at[1],
        device_id={"layer": other}, device_id_type=MESH,
    )
    exchange.start()

    def picks(row):
        count = jnp.int32(0)
        found = [jnp.int32(0)] * PICKS
        for j in range(n):
            here = pat[row, j]
            for s in range(PICKS):
                found[s] = jnp.where((here == 1) & (count == s), j, found[s])
            count = count + here
        return found

    for table in tables:
        table.wait()
    near = picks(g)
    flag = branch[g]
    def choose(h, gp):
        for s in range(PICKS):
            piece = buf[h, gp, :PICKS * HALF, :]
            sel[s, h] = jnp.where(near[s] == gp, piece, sel[s, h])

    def piece_copy(way, target, h, gp, q):
        return pltpu.make_async_remote_copy(
            src_ref=buf.at[h, gp, CHUNKS[q]], dst_ref=buf.at[h, gp, CHUNKS[q]],
            send_sem=send_sem.at[way, gp, q], recv_sem=recv_sem.at[h, gp, q],
            device_id=target, device_id_type=MESH,
        )

    def to_up(gp, q):
        return piece_copy(0, {"grid": up}, l, gp, q)

    def to_down(gp, q):
        return piece_copy(1, {"grid": down}, l, gp, q)

    def to_across(gp, q):
        return piece_copy(2, {"grid": across}, l, gp, q)

    def to_core(gp, q):
        return piece_copy(3, {"layer": other}, l, gp, q)

    def arrived(h, gp, q):
        piece_copy(3, {"layer": other}, h, gp, q).wait_recv()

    load_half.wait()
    exchange.wait()

    squares = jnp.zeros((8, BLOCK), jnp.float32)
    for s in range(PICKS):
        block = jnp.zeros((HALF, BLOCK), jnp.float32)
        for j in range(n):
            block = jnp.where(near[s] == j, full[:, j * BLOCK:(j + 1) * BLOCK], block)
        buf[l, g, s * HALF:(s + 1) * HALF, :] = block
        squares = squares + jnp.sum((block * block).reshape(HALF // 8, 8, BLOCK), axis=0)
    diagonal = full[:, pl.ds(pl.multiple_of(g * BLOCK, BLOCK), BLOCK)]
    at_row = lax.broadcasted_iota(jnp.int32, (HALF, BLOCK), 0) + l * HALF
    at_col = lax.broadcasted_iota(jnp.int32, (HALF, BLOCK), 1)
    diagonal = jnp.where(at_row == at_col, diagonal, 0.0)
    twice = 2.0 * jnp.sum(diagonal.reshape(HALF // 8, 8, BLOCK), axis=0)
    buf[l, g, PICKS * HALF:, :] = jnp.where(flag == 1, twice - squares, squares)

    for q in range(len(CHUNKS)):
        @pl.when(up_ok)
        def _(q=q):
            to_up(g, q).start()

        @pl.when(down_ok)
        def _(q=q):
            to_down(g, q).start()

        if ysize == 2:
            to_across(g, q).start()
        to_core(g, q).start()
    zero = jnp.int32(0)
    link = []
    for s in range(PICKS):
        link.append([
            sum((jnp.where(near[s] == j, pat[j, c], zero) for j in range(n)), zero)
            for c in range(n)
        ])
    sel[...] = jnp.zeros(sel.shape, jnp.float32)

    choose(l, g)

    def column(d, yy, act):
        def at(zz):
            act(zz * ysize + yy)

        if d == 0:
            at(z)
            return

        @pl.when(z - d >= 0)
        def _():
            at(z - d)

        @pl.when(z + d < zsize)
        def _():
            at(z + d)

    def across_arrives(gp):
        for q in range(len(CHUNKS)):
            arrived(l, gp, q)
            to_core(gp, q).start()
        choose(l, gp)

    def core_arrives(gp):
        for q in range(len(CHUNKS)):
            arrived(other, gp, q)
        choose(other, gp)

    def pass_on(gp, q, further, way):
        arrived(l, gp, q)

        @pl.when(further)
        def _():
            way(gp, q).start()

        if ysize == 2:
            to_across(gp, q).start()
        to_core(gp, q).start()

    for d in range(1, zsize + 1):
        if d < zsize:
            for q in range(len(CHUNKS)):
                @pl.when(z - d >= 0)
                def _(d=d, q=q):
                    pass_on((z - d) * ysize + y, q, up_ok, to_up)

                @pl.when(z + d < zsize)
                def _(d=d, q=q):
                    pass_on((z + d) * ysize + y, q, down_ok, to_down)

            column(d, y, functools.partial(choose, l))

        if ysize == 2:
            column(d - 1, 1 - y, across_arrives)
        column(d - 1, y, core_arrives)
        if ysize == 2 and d > 1:
            column(d - 2, 1 - y, core_arrives)
    if ysize == 2:
        column(zsize - 1, 1 - y, core_arrives)
    load_all.wait()

    total = jnp.zeros((8, BLOCK), jnp.float32)
    for gp in range(n):
        for h in range(2):
            total = total + buf[h, gp, PICKS * HALF:, :]
    occ[0] = jnp.sum(total) * (1.0 / (n * BLOCK))

    def split(value):
        high = value.astype(jnp.bfloat16)
        return high, (value - high.astype(jnp.float32)).astype(jnp.bfloat16)

    for s in range(PICKS):
        count = zero
        counts = []
        for c in range(n):
            counts.append(count)
            count = count + link[s][c]
        for c in range(per):
            here = jnp.where(l == 0, link[s][c], link[s][per + c])
            slot = jnp.where(l == 0, counts[c], counts[per + c])
            slot = jnp.where(here == 1, slot, PICKS)
            for h in range(2):
                block = jnp.zeros((HALF, BLOCK), jnp.float32)
                for q in range(PICKS):
                    block = jnp.where(slot == q, sel[s, h, q * HALF:(q + 1) * HALF, :], block)
                high, low = split(block)
                rows = slice(s * BLOCK + h * HALF, s * BLOCK + (h + 1) * HALF)
                bhi[rows, c * BLOCK:(c + 1) * BLOCK] = high
                blo[rows, c * BLOCK:(c + 1) * BLOCK] = low

    ahi, alo = [], []
    for s in range(PICKS):
        block = jnp.concatenate(
            [buf[h, g, s * HALF:(s + 1) * HALF, :] for h in range(2)], axis=0
        )
        high, low = split(block)
        ahi.append(high)
        alo.append(low)
    ahi = jnp.concatenate(ahi, axis=1)
    alo = jnp.concatenate(alo, axis=1)
    dot = functools.partial(jnp.dot, preferred_element_type=jnp.float32)
    wide = min(cols, 512)
    for w in range(cols // wide):
        span = slice(w * wide, (w + 1) * wide)
        high, low = bhi[:, span], blo[:, span]
        product = dot(ahi, high) + (dot(ahi, low) + dot(alo, high))
        for i in range(wide // BLOCK):
            c = w * (wide // BLOCK) + i
            col = slice(c * BLOCK, (c + 1) * BLOCK)
            part = product[:, i * BLOCK:(i + 1) * BLOCK]
            masked = jnp.where(pat[g, l * per + c] == 1, mine[:, col], 0.0)
            chosen = jnp.where(flag == 1, 2.0 * masked - part, part)
            out[:, col] = jnp.where(keep[g, l * per + c] == 1, chosen, 0.0)

    for gp in range(n):
        zz, yy = gp // ysize, gp % ysize
        for q in range(len(CHUNKS)):
            to_core(gp, q).wait_send()

            @pl.when((yy == y) & (zz <= z) & up_ok)
            def _(gp=gp, q=q):
                to_up(gp, q).wait_send()

            @pl.when((yy == y) & (zz >= z) & down_ok)
            def _(gp=gp, q=q):
                to_down(gp, q).wait_send()

            if ysize == 2:
                @pl.when(yy == y)
                def _(gp=gp, q=q):
                    to_across(gp, q).wait_send()


def shards(zsize, ysize, density, pattern, branch, keep_blocks):
    rows, cols = density.shape
    n = zsize * ysize
    smem = pl.BlockSpec(memory_space=pltpu.SMEM)
    return pl.pallas_call(
        functools.partial(kernel, zsize, ysize),
        out_shape=(
            pltpu.VMEM((rows, cols), jnp.float32),
            jax.ShapeDtypeStruct((1,), jnp.float32),
        ),
        in_specs=[pl.BlockSpec(memory_space=pltpu.HBM)] * 4,
        out_specs=(pl.BlockSpec(memory_space=pltpu.VMEM), smem),
        scratch_shapes=[
            pltpu.SMEM(pattern.shape, jnp.int32),
            pltpu.SMEM(branch.shape, jnp.int32),
            pltpu.SMEM(keep_blocks.shape, jnp.int32),
            pltpu.VMEM((HALF, 2 * cols), jnp.float32),
            pltpu.VMEM((rows, cols), jnp.float32),
            pltpu.VMEM((2, n, PICKS * HALF + 8, BLOCK), jnp.float32),
            pltpu.VMEM((PICKS, 2, PICKS * HALF, BLOCK), jnp.float32),
            pltpu.VMEM((PICKS * BLOCK, cols), jnp.bfloat16),
            pltpu.VMEM((PICKS * BLOCK, cols), jnp.bfloat16),
            pltpu.SemaphoreType.DMA((5,)),
            pltpu.SemaphoreType.DMA((2,)),
            pltpu.SemaphoreType.DMA((4, n, len(CHUNKS))),
            pltpu.SemaphoreType.DMA((2, n, len(CHUNKS))),
        ],
        compiler_params=pltpu.CompilerParams(
            collective_id=0, has_side_effects=True, vmem_limit_bytes=40 * 1024 * 1024
        ),
        name="sp2",
    )(*(pltpu.with_memory_space_constraint(v, pltpu.HBM) for v in (pattern, branch, keep_blocks, density)))


def solution(mesh):
    n = mesh.shape["grid"]
    ysize = 2 if n == 8 else 1
    placed = (P(("groups", "grid"), "layer"), P(), P(), P())
    return jax.shard_map(
        functools.partial(shards, n // ysize, ysize),
        mesh=mesh,
        in_specs=placed,
        out_specs=(P(("groups", "grid"), "layer"), P("groups")),
        check_vma=False,
    )
```

```python
import functools

import jax
import jax.numpy as jnp
from jax import lax
from jax.experimental import pallas as pl
from jax.experimental.pallas import tpu as pltpu
from jax.sharding import PartitionSpec as P

BLOCK = 128
HALF = BLOCK // 2
PICKS = 3
CHUNKS = (slice(0, 96), slice(96, PICKS * HALF + 8))
MESH = pl.DeviceIdType.MESH


def kernel(
    zsize, ysize, pat_in, branch_in, keep_in, x, out, occ,
    pat, branch, keep,
    full, mine, buf, sel, bhi, blo, local_sem, ex_sem, send_sem, recv_sem,
):
    n = zsize * ysize
    cols = x.shape[1]
    per = cols // BLOCK
    g = lax.axis_index("grid")
    l = lax.axis_index("layer")
    other = 1 - l
    z = g // ysize
    y = g % ysize

    own_cols = pl.ds(pl.multiple_of(l * cols, BLOCK), cols)
    own_rows = pl.ds(pl.multiple_of(l * HALF, 8), HALF)
    other_rows = pl.ds(pl.multiple_of(other * HALF, 8), HALF)
    load_half = pltpu.make_async_copy(x.at[own_rows, :], full.at[:, own_cols], local_sem.at[0])
    load_half.start()
    load_all = pltpu.make_async_copy(x, mine, local_sem.at[1])
    load_all.start()

    tables = [
        pltpu.make_async_copy(source, held, local_sem.at[2 + i])
        for i, (source, held) in enumerate(((pat_in, pat), (branch_in, branch), (keep_in, keep)))
    ]
    for table in tables:
        table.start()

    up_ok, down_ok = z + 1 < zsize, z > 0
    up, down = (z + 1) * ysize + y, (z - 1) * ysize + y
    across = z * ysize + (1 - y)

    barrier = pltpu.get_barrier_semaphore()
    pl.semaphore_signal(barrier, inc=1, device_id={"layer": other}, device_id_type=MESH)
    if ysize == 2:
        pl.semaphore_signal(barrier, inc=1, device_id={"grid": across}, device_id_type=MESH)

    @pl.when(up_ok)
    def _():
        pl.semaphore_signal(barrier, inc=1, device_id={"grid": up}, device_id_type=MESH)

    @pl.when(down_ok)
    def _():
        pl.semaphore_signal(barrier, inc=1, device_id={"grid": down}, device_id_type=MESH)

    peers = ysize + up_ok.astype(jnp.int32) + down_ok.astype(jnp.int32)
    pl.semaphore_wait(barrier, peers)

    exchange = pltpu.make_async_remote_copy(
        src_ref=x.at[other_rows, :], dst_ref=full.at[:, own_cols],
        send_sem=ex_sem.at[0], recv_sem=ex_sem.at[1],
        device_id={"layer": other}, device_id_type=MESH,
    )
    exchange.start()

    def picks(row):
        count = jnp.int32(0)
        found = [jnp.int32(0)] * PICKS
        for j in range(n):
            here = pat[row, j]
            for s in range(PICKS):
                found[s] = jnp.where((here == 1) & (count == s), j, found[s])
            count = count + here
        return found

    for table in tables:
        table.wait()
    near = picks(g)
    flag = branch[g]
    def choose(h, gp):
        for s in range(PICKS):
            piece = buf[h, gp, :PICKS * HALF, :]
            sel[s, h] = jnp.where(near[s] == gp, piece, sel[s, h])

    def piece_copy(way, target, h, gp, q):
        return pltpu.make_async_remote_copy(
            src_ref=buf.at[h, gp, CHUNKS[q]], dst_ref=buf.at[h, gp, CHUNKS[q]],
            send_sem=send_sem.at[way, gp, q], recv_sem=recv_sem.at[h, gp, q],
            device_id=target, device_id_type=MESH,
        )

    def to_up(gp, q):
        return piece_copy(0, {"grid": up}, l, gp, q)

    def to_down(gp, q):
        return piece_copy(1, {"grid": down}, l, gp, q)

    def to_across(gp, q):
        return piece_copy(2, {"grid": across}, l, gp, q)

    def to_core(gp, q):
        return piece_copy(3, {"layer": other}, l, gp, q)

    def arrived(h, gp, q):
        piece_copy(3, {"layer": other}, h, gp, q).wait_recv()

    load_half.wait()
    exchange.wait()

    squares = jnp.zeros((8, BLOCK), jnp.float32)
    for s in range(PICKS):
        block = jnp.zeros((HALF, BLOCK), jnp.float32)
        for j in range(n):
            block = jnp.where(near[s] == j, full[:, j * BLOCK:(j + 1) * BLOCK], block)
        buf[l, g, s * HALF:(s + 1) * HALF, :] = block
        squares = squares + jnp.sum((block * block).reshape(HALF // 8, 8, BLOCK), axis=0)
    diagonal = full[:, pl.ds(pl.multiple_of(g * BLOCK, BLOCK), BLOCK)]
    at_row = lax.broadcasted_iota(jnp.int32, (HALF, BLOCK), 0) + l * HALF
    at_col = lax.broadcasted_iota(jnp.int32, (HALF, BLOCK), 1)
    diagonal = jnp.where(at_row == at_col, diagonal, 0.0)
    twice = 2.0 * jnp.sum(diagonal.reshape(HALF // 8, 8, BLOCK), axis=0)
    buf[l, g, PICKS * HALF:, :] = jnp.where(flag == 1, twice - squares, squares)

    for q in range(len(CHUNKS)):
        @pl.when(up_ok)
        def _(q=q):
            to_up(g, q).start()

        @pl.when(down_ok)
        def _(q=q):
            to_down(g, q).start()

        if ysize == 2:
            to_across(g, q).start()
        to_core(g, q).start()
    zero = jnp.int32(0)
    link = []
    for s in range(PICKS):
        link.append([
            sum((jnp.where(near[s] == j, pat[j, c], zero) for j in range(n)), zero)
            for c in range(n)
        ])
    sel[...] = jnp.zeros(sel.shape, jnp.float32)

    choose(l, g)

    def column(d, yy, act):
        def at(zz):
            act(zz * ysize + yy)

        if d == 0:
            at(z)
            return

        @pl.when(z - d >= 0)
        def _():
            at(z - d)

        @pl.when(z + d < zsize)
        def _():
            at(z + d)

    def across_arrives(gp):
        for q in range(len(CHUNKS)):
            arrived(l, gp, q)
            to_core(gp, q).start()
        choose(l, gp)

    def core_arrives(gp):
        for q in range(len(CHUNKS)):
            arrived(other, gp, q)
        choose(other, gp)

    def pass_on(gp, q, further, way):
        arrived(l, gp, q)

        @pl.when(further)
        def _():
            way(gp, q).start()

        if ysize == 2:
            to_across(gp, q).start()
        to_core(gp, q).start()

    for d in range(1, zsize + 1):
        if d < zsize:
            for q in range(len(CHUNKS)):
                @pl.when(z - d >= 0)
                def _(d=d, q=q):
                    pass_on((z - d) * ysize + y, q, up_ok, to_up)

                @pl.when(z + d < zsize)
                def _(d=d, q=q):
                    pass_on((z + d) * ysize + y, q, down_ok, to_down)


        if ysize == 2:
            column(d - 1, 1 - y, across_arrives)
        if d < zsize:
            column(d, y, functools.partial(choose, l))
        column(d - 1, y, core_arrives)
        if ysize == 2 and d > 1:
            column(d - 2, 1 - y, core_arrives)
    if ysize == 2:
        column(zsize - 1, 1 - y, core_arrives)
    load_all.wait()

    total = jnp.zeros((8, BLOCK), jnp.float32)
    for gp in range(n):
        for h in range(2):
            total = total + buf[h, gp, PICKS * HALF:, :]
    occ[0] = jnp.sum(total) * (1.0 / (n * BLOCK))

    def split(value):
        high = value.astype(jnp.bfloat16)
        return high, (value - high.astype(jnp.float32)).astype(jnp.bfloat16)

    for s in range(PICKS):
        count = zero
        counts = []
        for c in range(n):
            counts.append(count)
            count = count + link[s][c]
        for c in range(per):
            here = jnp.where(l == 0, link[s][c], link[s][per + c])
            slot = jnp.where(l == 0, counts[c], counts[per + c])
            slot = jnp.where(here == 1, slot, PICKS)
            for h in range(2):
                block = jnp.zeros((HALF, BLOCK), jnp.float32)
                for q in range(PICKS):
                    block = jnp.where(slot == q, sel[s, h, q * HALF:(q + 1) * HALF, :], block)
                high, low = split(block)
                rows = slice(s * BLOCK + h * HALF, s * BLOCK + (h + 1) * HALF)
                bhi[rows, c * BLOCK:(c + 1) * BLOCK] = high
                blo[rows, c * BLOCK:(c + 1) * BLOCK] = low

    ahi, alo = [], []
    for s in range(PICKS):
        block = jnp.concatenate(
            [buf[h, g, s * HALF:(s + 1) * HALF, :] for h in range(2)], axis=0
        )
        high, low = split(block)
        ahi.append(high)
        alo.append(low)
    ahi = jnp.concatenate(ahi, axis=1)
    alo = jnp.concatenate(alo, axis=1)
    dot = functools.partial(jnp.dot, preferred_element_type=jnp.float32)
    wide = min(cols, 512)
    for w in range(cols // wide):
        span = slice(w * wide, (w + 1) * wide)
        high, low = bhi[:, span], blo[:, span]
        product = dot(ahi, high) + (dot(ahi, low) + dot(alo, high))
        for i in range(wide // BLOCK):
            c = w * (wide // BLOCK) + i
            col = slice(c * BLOCK, (c + 1) * BLOCK)
            part = product[:, i * BLOCK:(i + 1) * BLOCK]
            masked = jnp.where(pat[g, l * per + c] == 1, mine[:, col], 0.0)
            chosen = jnp.where(flag == 1, 2.0 * masked - part, part)
            out[:, col] = jnp.where(keep[g, l * per + c] == 1, chosen, 0.0)

    for gp in range(n):
        zz, yy = gp // ysize, gp % ysize
        for q in range(len(CHUNKS)):
            to_core(gp, q).wait_send()

            @pl.when((yy == y) & (zz <= z) & up_ok)
            def _(gp=gp, q=q):
                to_up(gp, q).wait_send()

            @pl.when((yy == y) & (zz >= z) & down_ok)
            def _(gp=gp, q=q):
                to_down(gp, q).wait_send()

            if ysize == 2:
                @pl.when(yy == y)
                def _(gp=gp, q=q):
                    to_across(gp, q).wait_send()


def shards(zsize, ysize, density, pattern, branch, keep_blocks):
    rows, cols = density.shape
    n = zsize * ysize
    smem = pl.BlockSpec(memory_space=pltpu.SMEM)
    return pl.pallas_call(
        functools.partial(kernel, zsize, ysize),
        out_shape=(
            pltpu.VMEM((rows, cols), jnp.float32),
            jax.ShapeDtypeStruct((1,), jnp.float32),
        ),
        in_specs=[pl.BlockSpec(memory_space=pltpu.HBM)] * 4,
        out_specs=(pl.BlockSpec(memory_space=pltpu.VMEM), smem),
        scratch_shapes=[
            pltpu.SMEM(pattern.shape, jnp.int32),
            pltpu.SMEM(branch.shape, jnp.int32),
            pltpu.SMEM(keep_blocks.shape, jnp.int32),
            pltpu.VMEM((HALF, 2 * cols), jnp.float32),
            pltpu.VMEM((rows, cols), jnp.float32),
            pltpu.VMEM((2, n, PICKS * HALF + 8, BLOCK), jnp.float32),
            pltpu.VMEM((PICKS, 2, PICKS * HALF, BLOCK), jnp.float32),
            pltpu.VMEM((PICKS * BLOCK, cols), jnp.bfloat16),
            pltpu.VMEM((PICKS * BLOCK, cols), jnp.bfloat16),
            pltpu.SemaphoreType.DMA((5,)),
            pltpu.SemaphoreType.DMA((2,)),
            pltpu.SemaphoreType.DMA((4, n, len(CHUNKS))),
            pltpu.SemaphoreType.DMA((2, n, len(CHUNKS))),
        ],
        compiler_params=pltpu.CompilerParams(
            collective_id=0, has_side_effects=True, vmem_limit_bytes=40 * 1024 * 1024
        ),
        name="sp2",
    )(*(pltpu.with_memory_space_constraint(v, pltpu.HBM) for v in (pattern, branch, keep_blocks, density)))


def solution(mesh):
    n = mesh.shape["grid"]
    ysize = 2 if n == 8 else 1
    placed = (P(("groups", "grid"), "layer"), P(), P(), P())
    return jax.shard_map(
        functools.partial(shards, n // ysize, ysize),
        mesh=mesh,
        in_specs=placed,
        out_specs=(P(("groups", "grid"), "layer"), P("groups")),
        check_vma=False,
    )
```
